32 devices in a mesh: groups: 1, side: 2 (over core), dev: 16 (over z, y, x).
Axes of the slice: x: 2, y: 2, z: 4, core: 2. Of those that a mesh axis runs over, the one named last changes fastest.
Arguments:
- tokens: bfloat16 [256, 4096], P(('groups', 'side', 'dev')), may hold values from -6 to 6
- norm_gain: float32 [4096], replicated, may hold values from 0.1 to 1.9
- expert_ids: int32 [256, 8], P(('groups', 'side', 'dev')), may hold values from 0 to 15, all different within a row; in each aligned block of 8 rows (0 to 7, 8 to 15, ...) at most 8 rows name the same one
- route_weight: float32 [256, 8], P(('groups', 'side', 'dev')), may hold values from 0.05 to 1
- placement: int32 [16], replicated, may hold values from 0 to 15, each once
- w_gate: bfloat16 [16, 4096, 768], P('dev', None, 'side'), may hold values from -0.09375 to 0.09375
- w_up: bfloat16 [16, 4096, 768], P('dev', None, 'side'), may hold values from -0.09375 to 0.09375
- w_down: bfloat16 [16, 768, 4096], P('dev', 'side'), may hold values from -0.21875 to 0.21875
Outputs:
- combined: bfloat16 [256, 4096], P(('groups', 'side', 'dev'))
The draws below stay inside these ranges and needn't reach their ends.
Inputs may be any that keep to these rules, and one draw needn't show every extreme that they name: `expert_ids`: each row names 8 different experts; among the rows of one device no expert is named more than 8 times. `placement`: A permutation of the weight slots.
All inputs are finite; a program needn't handle non-finite values.
Results may differ from the reference program's by a relative error of at most 0.007.
Values may be sent and summed in bfloat16 or wider, within the bound.
No kernel may reach another device: no remote copies, remote signals or barrier semaphores. Data moves between devices by JAX's collectives and lax.ppermute only.
A program may use at most 64 MiB of HBM per device.

```python
import math
import jax
import jax.numpy as jnp
import numpy as np
from jax import lax

D = 4096
FF = 768
TOP = 8
TOK_DEV = 8
EXPERTS = 16
CAP = 8
TOKENS = 256
N_SIDE = 2
N_DEV = 16


def block_scale(stream_key, shape, split, least, top_value):
    def one(position, parts):
        heights = jax.random.uniform(jax.random.fold_in(jax.random.fold_in(stream_key, 6), position), (parts,), jnp.float32, least / len(split), top_value / len(split))
        return jnp.repeat(jnp.exp(heights), shape[position] // parts).reshape((-1,) + (1,) * (len(shape) - position - 1))

    gain = one(*split[0])
    for cut in split[1:]:
        gain = gain * one(*cut)
    return gain


def assign_block(own_key, own, number, rows, amount, top, reach, slope):
    order = jax.random.permutation(own_key, amount)
    packed, common = shares(amount, rows * top, reach, slope, True), shares(amount, rows * top, reach, slope, False)
    places = jnp.arange(amount)

    def named(lengths, offset_by):
        used = int((lengths > 0).sum())
        fixed = max(1, used // 4)
        shifted = fixed + (places - fixed + offset_by * (used - fixed)) % max(1, amount - fixed)
        return jnp.zeros((amount,), jnp.int32).at[order[jnp.where(places < fixed, places, shifted)]].set(jnp.asarray(lengths, jnp.int32))

    lengths = jnp.where(number % 4 == 0, named(packed, number // 4), named(common, number - number // 4 - 1))
    mixed = jax.random.permutation(jax.random.fold_in(own, 3), amount)
    donor, taker = mixed[0:amount // 2 * 2:2], mixed[1:amount // 2 * 2:2]
    slack = jnp.minimum(lengths[donor] - 1, reach - lengths[taker]) // 2
    slack = jnp.where((donor == order[0]) | (taker == order[0]) | (lengths[taker] == 0), 0, jnp.maximum(slack, 0))
    shifted = jax.random.randint(jax.random.fold_in(own, 4), (amount // 2,), 0, 1 << 20) % (slack + 1)
    lengths = lengths.at[donor].add(-shifted).at[taker].add(shifted)
    members = jnp.searchsorted(jnp.cumsum(lengths), jnp.arange(rows * top), side="right").astype(jnp.int32)
    grid = members.reshape(top, rows).T
    grid = grid[jax.random.permutation(jax.random.fold_in(own, 1), rows)]
    offset_by = jax.random.randint(jax.random.fold_in(own, 2), (rows, 1), 0, top)
    return jnp.take_along_axis(grid, (jnp.arange(top)[None, :] + offset_by) % top, axis=1)


def shares(count, total, most, slope, full):
    portions = [(1 << 20) // math.isqrt(rank ** slope) + 1 for rank in range(1, count + 1)]
    largest = most if full else min(most, max(-(-total // count), total * portions[0] // sum(portions)))
    least = 1 if total - largest >= count - 1 else 0
    given, rest = [largest] + [least] * (count - 1), total - largest - least * (count - 1)
    while rest > 0:
        free = [i for i in range(1, count) if given[i] < largest] or [i for i in range(1, count) if given[i] < most]
        whole, left = sum([portions[i] for i in free]), rest
        for i in free:
            addition = min(most - given[i], max(1, left * portions[i] // whole), rest)
            given[i] = given[i] + addition
            rest = rest - addition
    return np.array(given)


def scatter_about(rng, shape, width, reach, split=(), held_as=jnp.bfloat16):
    loudness = block_scale(rng, shape, split, -0.22, 0.18) if split else 1.0
    values = jax.random.normal(rng, shape, jnp.float32) * width * loudness
    return jnp.minimum(jnp.maximum(values, -reach), reach).astype(held_as)


def setup_inputs(seed: int = 0, part: int = 0) -> dict:
    key_list = jax.random.split(jax.random.key(seed), 9)
    own_keys = jax.random.split(jax.random.fold_in(key_list[8], part), 9)
    tokens = scatter_about(own_keys[0], (TOKENS, D), 1.0, 6.0, ((0, 32),))
    norm_gain = jnp.clip(1.0 + 0.18 * jax.random.normal(key_list[1], (D,), jnp.float32), 0.1, 1.9)
    expert_ids_keys = jax.random.split(jax.random.fold_in(own_keys[2], 1), TOKENS // TOK_DEV)
    expert_ids_turns = jax.random.permutation(jax.random.fold_in(own_keys[2], 3), TOKENS // TOK_DEV)
    expert_ids = jax.vmap(lambda own, number: assign_block(jax.random.fold_in(own_keys[2], 2), own, number, TOK_DEV, EXPERTS, TOP, CAP, 2))(expert_ids_keys, expert_ids_turns).reshape((TOKENS, TOP))
    route_weight = jnp.clip(jnp.exp(math.log(1.0) - 2.9957323 * jax.random.uniform(own_keys[3], (TOKENS, TOP), jnp.float32) ** block_scale(own_keys[3], (TOKENS, TOP), ((0, 32),), -0.2, 0.2)), 0.05, 1.0)
    placement = jax.random.permutation(key_list[4], EXPERTS).astype(jnp.int32)
    w_gate = scatter_about(key_list[5], (EXPERTS, D, FF), D ** -0.5, 0.09375, ((0, 16), (2, 2)))
    w_up = scatter_about(key_list[6], (EXPERTS, D, FF), D ** -0.5, 0.09375, ((0, 16), (2, 2)))
    w_down = scatter_about(key_list[7], (EXPERTS, FF, D), FF ** -0.5, 0.21875, ((0, 16), (1, 2)))
    return dict(tokens=tokens, norm_gain=norm_gain, expert_ids=expert_ids, route_weight=route_weight, placement=placement, w_gate=w_gate, w_up=w_up, w_down=w_down)


def reference(tokens, norm_gain, expert_ids, route_weight, placement, w_gate, w_up, w_down):
    values = tokens.astype(jnp.float32)
    scale = lax.rsqrt(lax.optimization_barrier(jnp.mean(values * values, axis=-1, keepdims=True)) + 1e-06)
    normed = (values * scale * norm_gain).astype(jnp.bfloat16)
    owner_slot = placement[expert_ids.reshape(-1)].astype(jnp.int32)
    token_of = (jnp.arange(TOKENS * TOP) // TOP).astype(jnp.int32)
    flat_weight = route_weight.reshape(-1)
    limit = N_SIDE * N_DEV * CAP

    def visit(total, index):
        chosen = owner_slot == index
        picked = jnp.nonzero(chosen, size=limit, fill_value=0)[0].astype(jnp.int32)
        live = (jnp.arange(limit) < jnp.sum(chosen.astype(jnp.int32))).astype(jnp.float32)
        source = token_of[picked]
        gathered = normed[source]
        gate = jnp.dot(gathered, w_gate[index], preferred_element_type=jnp.float32)
        upward = jnp.dot(gathered, w_up[index], preferred_element_type=jnp.float32)
        hidden = (jax.nn.silu(gate) * upward).astype(jnp.bfloat16)
        result = jnp.dot(hidden, w_down[index], preferred_element_type=jnp.float32).astype(jnp.bfloat16)
        scaled = result.astype(jnp.float32) * (flat_weight[picked] * live)[:, None]
        return (total.at[source].add(scaled), index)
    start = jnp.zeros((TOKENS, D), jnp.float32)
    total, visited = lax.scan(visit, start, jnp.arange(EXPERTS).astype(jnp.int32))
    return total.astype(jnp.bfloat16)
```

```python
import functools

import jax
import jax.numpy as jnp
from jax import lax
from jax.experimental import pallas as pl
from jax.experimental.pallas import tpu as pltpu
from jax.sharding import PartitionSpec as P


def swap(block, axis, offset):
    count = lax.axis_size(axis)
    return lax.ppermute(block, axis, [(i, i ^ offset) for i in range(count)])


def prepare_kernel(slots, tok_ref, gain_ref, ids_ref, weight_ref, placement_ref, out_ref):
    width = tok_ref.shape[1]
    values = tok_ref[...].astype(jnp.float32)
    scale = lax.rsqrt(jnp.mean(values * values, axis=-1, keepdims=True) + 1e-06)
    out_ref[:, :width] = (values * scale * gain_ref[...].reshape(1, width)).astype(jnp.bfloat16)
    ids = ids_ref[...]
    slot = jnp.zeros_like(ids)
    for expert in range(placement_ref.shape[0]):
        slot = jnp.where(ids == expert, placement_ref[expert], slot)
    lane = lax.broadcasted_iota(jnp.int32, (ids.shape[0], out_ref.shape[1] - width), 1)
    place = lax.rem(lane, slots)
    section = lax.div(lane, slots)
    mixing = jnp.zeros(lane.shape, jnp.float32)
    for k in range(ids.shape[1]):
        mixing += jnp.where(place == slot[:, k : k + 1], weight_ref[:, k : k + 1], 0.0)
    high = mixing.astype(jnp.bfloat16)
    rest = mixing - high.astype(jnp.float32)
    middle = rest.astype(jnp.bfloat16)
    low = rest - middle.astype(jnp.float32)
    parts = jnp.where(
        section == 0,
        high.astype(jnp.float32),
        jnp.where(section == 1, middle.astype(jnp.float32), jnp.where(section == 2, low, 0.0)),
    )
    out_ref[:, width:] = parts.astype(jnp.bfloat16)


def prepare(tokens, norm_gain, expert_ids, route_weight, placement, slots, extra):
    count, width = tokens.shape
    vmem = pl.BlockSpec(memory_space=pltpu.VMEM)
    return pl.pallas_call(
        functools.partial(prepare_kernel, slots),
        out_shape=jax.ShapeDtypeStruct((count, width + extra), jnp.bfloat16),
        in_specs=[vmem, vmem, vmem, vmem, pl.BlockSpec(memory_space=pltpu.SMEM)],
        out_specs=vmem,
    )(tokens, norm_gain, expert_ids, route_weight, placement)


def hidden_rows(rows, w_gate, w_up):
    gate = jnp.dot(rows, w_gate, preferred_element_type=jnp.float32)
    upward = jnp.dot(rows, w_up, preferred_element_type=jnp.float32)
    return (jax.nn.silu(gate) * upward).astype(jnp.bfloat16)


def body(tokens, norm_gain, expert_ids, route_weight, placement, w_gate, w_up, w_down):
    count, width = tokens.shape
    owners = lax.axis_size("dev")
    me = lax.axis_index("dev")
    half = width // 2
    extra = -(-3 * owners // 128) * 128
    packed = prepare(tokens, norm_gain, expert_ids, route_weight, placement, owners, extra)
    cold = list(range(4, owners, 4))
    column = jnp.concatenate([packed] + [swap(packed, "dev", r) for r in cold])
    span = column.shape[0]
    along_x = swap(column, "dev", 1)
    along_y = swap(column, "dev", 2)
    diag = jnp.concatenate(
        [swap(along_y[:, :half], "dev", 1), swap(along_x[:, half:], "dev", 2)], axis=1
    )
    own = jnp.concatenate([column, along_x, along_y, diag])
    other = swap(own, "side", 1)

    def routed(rows):
        chosen = lax.rem(lax.broadcasted_iota(jnp.int32, (1, extra), 1), owners) == me
        weight = jnp.sum(
            jnp.where(chosen, rows[:, width:].astype(jnp.float32), 0.0), axis=1, keepdims=True
        )
        hidden = hidden_rows(rows[:, :width], w_gate[0], w_up[0])
        return jnp.dot(hidden, w_down[0], preferred_element_type=jnp.float32) * weight

    away = routed(other).astype(jnp.bfloat16)
    total = routed(own) + swap(away, "side", 1).astype(jnp.float32)
    s_own, s_x, s_y, s_diag = (total[i * span : (i + 1) * span] for i in range(4))

    def send(value, offset):
        return swap(value.astype(jnp.bfloat16), "dev", offset).astype(jnp.float32)

    from_y = send(s_diag[:, :half], 2)
    from_x = send(s_diag[:, half:], 1)
    s_x = jnp.concatenate([s_x[:, :half] + from_y, s_x[:, half:]], axis=1)
    s_y = jnp.concatenate([s_y[:, :half], s_y[:, half:] + from_x], axis=1)
    column_sum = s_own + send(s_x, 1) + send(s_y, 2)
    result = column_sum[:count]
    for i, r in enumerate(cold):
        result = result + send(column_sum[(i + 1) * count : (i + 2) * count], r)
    return result.astype(jnp.bfloat16)


def solution(mesh):
    in_specs = (
        P(("groups", "side", "dev"), None),
        P(),
        P(("groups", "side", "dev"), None),
        P(("groups", "side", "dev"), None),
        P(),
        P("dev", None, "side"),
        P("dev", None, "side"),
        P("dev", "side", None),
    )
    out_specs = P(("groups", "side", "dev"), None)
    return jax.shard_map(body, mesh=mesh, in_specs=in_specs, out_specs=out_specs, check_vma=False)
```

```python
import functools
import math

import jax
import jax.numpy as jnp
from jax import lax
from jax.experimental import pallas as pl
from jax.experimental.pallas import tpu as pltpu
from jax.sharding import PartitionSpec as P


def swap(block, axis, offset):
    count = lax.axis_size(axis)
    return lax.ppermute(block, axis, [(i, i ^ offset) for i in range(count)])


def prepare_kernel(slots, tok_ref, gain_ref, ids_ref, weight_ref, placement_ref, out_ref):
    width = tok_ref.shape[1]
    values = tok_ref[...].astype(jnp.float32)
    scale = lax.rsqrt(jnp.mean(values * values, axis=-1, keepdims=True) + 1e-06)
    out_ref[:, :width] = (values * scale * gain_ref[...].reshape(1, width)).astype(jnp.bfloat16)
    ids = ids_ref[...]
    slot = jnp.zeros_like(ids)
    for expert in range(placement_ref.shape[0]):
        slot = jnp.where(ids == expert, placement_ref[expert], slot)
    lane = lax.broadcasted_iota(jnp.int32, (ids.shape[0], out_ref.shape[1] - width), 1)
    place = lax.rem(lane, slots)
    section = lax.div(lane, slots)
    mixing = jnp.zeros(lane.shape, jnp.float32)
    for k in range(ids.shape[1]):
        mixing += jnp.where(place == slot[:, k : k + 1], weight_ref[:, k : k + 1], 0.0)
    high = mixing.astype(jnp.bfloat16)
    rest = mixing - high.astype(jnp.float32)
    middle = rest.astype(jnp.bfloat16)
    low = rest - middle.astype(jnp.float32)
    parts = jnp.where(
        section == 0,
        high.astype(jnp.float32),
        jnp.where(section == 1, middle.astype(jnp.float32), jnp.where(section == 2, low, 0.0)),
    )
    out_ref[:, width:] = parts.astype(jnp.bfloat16)


def prepare(tokens, norm_gain, expert_ids, route_weight, placement, slots, extra):
    count, width = tokens.shape
    vmem = pl.BlockSpec(memory_space=pltpu.VMEM)
    return pl.pallas_call(
        functools.partial(prepare_kernel, slots),
        out_shape=jax.ShapeDtypeStruct((count, width + extra), jnp.bfloat16),
        in_specs=[vmem, vmem, vmem, vmem, pl.BlockSpec(memory_space=pltpu.SMEM)],
        out_specs=vmem,
        compiler_params=pltpu.CompilerParams(vmem_limit_bytes=LIMIT),
    )(tokens, norm_gain, expert_ids, route_weight, placement)


VMEM = pl.BlockSpec(memory_space=pltpu.VMEM)
LIMIT = 56 * 1024 * 1024
ROOM = int(53.0 * 1024 * 1024)


def local_call(kernel, outs, *operands, hint=0):
    held = sum(math.prod(x.shape) * x.dtype.itemsize for x in operands)
    held += sum(math.prod(shape) * jnp.dtype(dtype).itemsize for shape, dtype in outs)
    return pl.pallas_call(
        kernel,
        out_shape=[jax.ShapeDtypeStruct(shape, dtype) for shape, dtype in outs],
        in_specs=[VMEM] * len(operands),
        out_specs=[VMEM] * len(outs),
        compiler_params=pltpu.CompilerParams(vmem_limit_bytes=min(LIMIT, 2 * held + (1 << 21))),
        cost_estimate=pl.CostEstimate(flops=0, bytes_accessed=hint or held, transcendentals=0),
    )(*operands)


def stack_kernel(*refs):
    out_ref = refs[-1]
    start = 0
    for ref in refs[:-1]:
        out_ref[start : start + ref.shape[0]] = ref[...]
        start += ref.shape[0]


def stack(*blocks):
    if len(blocks) == 1:
        return blocks[0]
    rows = sum(block.shape[0] for block in blocks)
    return local_call(
        stack_kernel, [((rows, blocks[0].shape[1]), blocks[0].dtype)], *blocks, hint=8 << 20
    )[0]


def turn(block, first, second):
    owners = lax.axis_size("dev")
    route = []
    for side, offset in enumerate((first, second)):
        route += [(side * owners + i, side * owners + (i ^ offset)) for i in range(owners)]
    return lax.ppermute(block, ("side", "dev"), route)


def expert_kernel(
    column_ref, near_ref, far_ref, mine_ref, other_ref, gate_ref, up_ref, down_ref,
    away_ref, keep_ref,
):
    span = mine_ref.shape[0]
    width = keep_ref.shape[1]
    extra = column_ref.shape[1] - width
    owners = lax.axis_size("dev")
    me = lax.axis_index("dev")
    step = min(width, 1024)

    def rows(start, size):
        columns = slice(start, start + size)
        return jnp.concatenate(
            [
                other_ref[:, columns],
                far_ref[:, columns],
                column_ref[span:, columns],
                mine_ref[:, columns],
                near_ref[:, columns],
                column_ref[:span, columns],
            ]
        )

    gate = up = 0.0
    for k in range(0, width, step):
        part = rows(k, step)
        gate += jnp.dot(part, gate_ref[0, k : k + step], preferred_element_type=jnp.float32)
        up += jnp.dot(part, up_ref[0, k : k + step], preferred_element_type=jnp.float32)
    hidden = (gate / (1.0 + jnp.exp(-gate)) * up).astype(jnp.bfloat16)
    lane = lax.broadcasted_iota(jnp.int32, (1, extra), 1)
    parts = rows(width, extra).astype(jnp.float32)
    weight = jnp.sum(jnp.where(lax.rem(lane, owners) == me, parts, 0.0), axis=1, keepdims=True)
    half = 4 * span
    for k in range(0, width, step):
        down = down_ref[0, :, k : k + step]
        value = jnp.dot(hidden, down, preferred_element_type=jnp.float32) * weight
        away_ref[:, k : k + step] = value[:half].astype(jnp.bfloat16)
        keep_ref[:, k : k + step] = value[half:]


def corner_kernel(keep_ref, got_ref, out_ref):
    span = out_ref.shape[0]
    out_ref[...] = (keep_ref[:span] + got_ref[:span].astype(jnp.float32)).astype(jnp.bfloat16)


def near_kernel(keep_ref, got_ref, corner_ref, out_ref):
    span = corner_ref.shape[0]
    total = keep_ref[span : 3 * span] + got_ref[span : 3 * span].astype(jnp.float32)
    out_ref[:span] = (total[:span] + corner_ref[...].astype(jnp.float32)).astype(jnp.bfloat16)
    out_ref[span:] = total[span:].astype(jnp.bfloat16)


def column_kernel(keep_ref, got_ref, near_ref, other_ref, *out_refs):
    count = out_refs[0].shape[0]
    base = 3 * other_ref.shape[0]
    for i, out_ref in enumerate(out_refs):
        rows = slice(i * count, (i + 1) * count)
        kept = slice(base + i * count, base + (i + 1) * count)
        total = keep_ref[kept] + got_ref[kept].astype(jnp.float32)
        total = total + near_ref[rows].astype(jnp.float32) + other_ref[rows].astype(jnp.float32)
        out_ref[...] = total.astype(out_ref.dtype)


def finish_kernel(first_ref, *refs):
    total = first_ref[...]
    for ref in refs[:-1]:
        total = total + ref[...].astype(jnp.float32)
    refs[-1][...] = total.astype(jnp.bfloat16)


def load_kernel(*refs):
    count = len(refs) // 2
    sources, targets, sem = refs[:count], refs[count:-1], refs[-1]
    copies = [pltpu.make_async_copy(*pair, sem.at[i]) for i, pair in enumerate(zip(sources, targets))]
    for copy in copies:
        copy.start()
    for copy in copies:
        copy.wait()


def load(*arrays):
    held = sum(math.prod(x.shape) * x.dtype.itemsize for x in arrays)
    return pl.pallas_call(
        load_kernel,
        out_shape=[jax.ShapeDtypeStruct(x.shape, x.dtype) for x in arrays],
        in_specs=[pl.BlockSpec(memory_space=pl.ANY)] * len(arrays),
        out_specs=[VMEM] * len(arrays),
        scratch_shapes=[pltpu.SemaphoreType.DMA((len(arrays),))],
        compiler_params=pltpu.CompilerParams(vmem_limit_bytes=ROOM - held),
        cost_estimate=pl.CostEstimate(flops=0, bytes_accessed=2 * held, transcendentals=0),
    )(*arrays)


def body(tokens, norm_gain, expert_ids, route_weight, placement, w_gate, w_up, w_down):
    count, width = tokens.shape
    owners = lax.axis_size("dev")
    extra = -(-3 * owners // 128) * 128
    bf16, f32 = jnp.bfloat16, jnp.float32
    packed = prepare(tokens, norm_gain, expert_ids, route_weight, placement, owners, extra)
    offsets = list(range(0, owners, 4))
    odd = [r for r in offsets if r // 4 % 2 == 1]
    even = [r for r in offsets if r // 4 % 2 == 0]
    groups = [group for group in (even, odd) if group]
    blocks = {r: swap(packed, "dev", r) for group in groups for r in group if r}
    *weights, blocks[0] = load(w_gate, w_up, w_down, packed)
    blocks, weights = lax.optimization_barrier((blocks, weights))
    pieces = []
    for group in groups:
        mine = stack(*[blocks[r] for r in group])
        span = mine.shape[0]
        column = stack(mine, swap(mine, "side", 1))
        near = turn(column, 1, 2)
        corner = turn(near[:span], 2, 1)
        far = swap(near, "side", 1)
        if pieces:
            corner = lax.optimization_barrier((corner, pieces[-1]))[0]
        pieces.append(
            local_call(
                expert_kernel,
                [((4 * span, width), bf16), ((4 * span, width), f32)],
                column, near, far, corner, swap(corner, "side", 1), *weights,
            )
        )
    sums = {}
    for group, (away, keep) in zip(groups, pieces):
        span = len(group) * count
        got = swap(away, "side", 1)
        corner = turn(local_call(corner_kernel, [((span, width), bf16)], keep, got)[0], 2, 1)
        near = local_call(near_kernel, [((2 * span, width), bf16)], keep, got, corner)[0]
        near = turn(near, 1, 2)
        totals = local_call(
            column_kernel,
            [((count, width), bf16 if r else f32) for r in group],
            keep, got, near, swap(near[span:], "side", 1),
        )
        for r, total in zip(group, totals):
            sums[r] = swap(total, "dev", r) if r else total
    return local_call(finish_kernel, [((count, width), bf16)], *[sums[r] for r in sorted(sums)])[0]


def solution(mesh):
    in_specs = (
        P(("groups", "side", "dev"), None),
        P(),
        P(("groups", "side", "dev"), None),
        P(("groups", "side", "dev"), None),
        P(),
        P("dev", None, "side"),
        P("dev", None, "side"),
        P("dev", "side", None),
    )
    out_specs = P(("groups", "side", "dev"), None)
    return jax.shard_map(body, mesh=mesh, in_specs=in_specs, out_specs=out_specs, check_vma=False)
```

```python
import functools
import math

import jax
import jax.numpy as jnp
from jax import lax
from jax.experimental import pallas as pl
from jax.experimental.pallas import tpu as pltpu
from jax.sharding import PartitionSpec as P


def swap(block, axis, offset):
    count = lax.axis_size(axis)
    return lax.ppermute(block, axis, [(i, i ^ offset) for i in range(count)])


def prepare_kernel(slots, tok_ref, gain_ref, ids_ref, weight_ref, placement_ref, out_ref):
    width = tok_ref.shape[1]
    values = tok_ref[...].astype(jnp.float32)
    scale = lax.rsqrt(jnp.mean(values * values, axis=-1, keepdims=True) + 1e-06)
    out_ref[:, :width] = (values * scale * gain_ref[...].reshape(1, width)).astype(jnp.bfloat16)
    ids = ids_ref[...]
    slot = jnp.zeros_like(ids)
    for expert in range(placement_ref.shape[0]):
        slot = jnp.where(ids == expert, placement_ref[expert], slot)
    lane = lax.broadcasted_iota(jnp.int32, (ids.shape[0], out_ref.shape[1] - width), 1)
    place = lax.rem(lane, slots)
    section = lax.div(lane, slots)
    mixing = jnp.zeros(lane.shape, jnp.float32)
    for k in range(ids.shape[1]):
        mixing += jnp.where(place == slot[:, k : k + 1], weight_ref[:, k : k + 1], 0.0)
    high = mixing.astype(jnp.bfloat16)
    rest = mixing - high.astype(jnp.float32)
    middle = rest.astype(jnp.bfloat16)
    low = rest - middle.astype(jnp.float32)
    parts = jnp.where(
        section == 0,
        high.astype(jnp.float32),
        jnp.where(section == 1, middle.astype(jnp.float32), jnp.where(section == 2, low, 0.0)),
    )
    out_ref[:, width:] = parts.astype(jnp.bfloat16)


def prepare(tokens, norm_gain, expert_ids, route_weight, placement, slots, extra):
    count, width = tokens.shape
    vmem = pl.BlockSpec(memory_space=pltpu.VMEM)
    return pl.pallas_call(
        functools.partial(prepare_kernel, slots),
        out_shape=jax.ShapeDtypeStruct((count, width + extra), jnp.bfloat16),
        in_specs=[vmem, vmem, vmem, vmem, pl.BlockSpec(memory_space=pltpu.SMEM)],
        out_specs=vmem,
        compiler_params=pltpu.CompilerParams(vmem_limit_bytes=LIMIT),
    )(tokens, norm_gain, expert_ids, route_weight, placement)


VMEM = pl.BlockSpec(memory_space=pltpu.VMEM)
LIMIT = 56 * 1024 * 1024
ROOM = int(53.0 * 1024 * 1024)


def local_call(kernel, outs, *operands, hint=0):
    held = sum(math.prod(x.shape) * x.dtype.itemsize for x in operands)
    held += sum(math.prod(shape) * jnp.dtype(dtype).itemsize for shape, dtype in outs)
    return pl.pallas_call(
        kernel,
        out_shape=[jax.ShapeDtypeStruct(shape, dtype) for shape, dtype in outs],
        in_specs=[VMEM] * len(operands),
        out_specs=[VMEM] * len(outs),
        compiler_params=pltpu.CompilerParams(vmem_limit_bytes=min(LIMIT, 2 * held + (1 << 21))),
        cost_estimate=pl.CostEstimate(flops=0, bytes_accessed=hint or held, transcendentals=0),
    )(*operands)


def stack_kernel(*refs):
    out_ref = refs[-1]
    start = 0
    for ref in refs[:-1]:
        out_ref[start : start + ref.shape[0]] = ref[...]
        start += ref.shape[0]


def stack(*blocks):
    if len(blocks) == 1:
        return blocks[0]
    rows = sum(block.shape[0] for block in blocks)
    return local_call(
        stack_kernel, [((rows, blocks[0].shape[1]), blocks[0].dtype)], *blocks, hint=8 << 20
    )[0]


def collect_kernel(column_ref, x_ref, y_ref, left_ref, right_ref, out_ref):
    span = column_ref.shape[0]
    half = left_ref.shape[1]
    out_ref[:span] = column_ref[...]
    out_ref[span : 2 * span] = x_ref[...]
    out_ref[2 * span : 3 * span] = y_ref[...]
    out_ref[3 * span :, :half] = left_ref[...]
    out_ref[3 * span :, half:] = right_ref[...]


def expert_kernel(own_ref, other_ref, gate_ref, up_ref, down_ref, away_ref, keep_ref):
    rows, width = keep_ref.shape
    extra = own_ref.shape[1] - width
    owners = lax.axis_size("dev")
    me = lax.axis_index("dev")
    step = min(width, 1024)
    gate = up = 0.0
    for k in range(0, width, step):
        part = jnp.concatenate([other_ref[:, k : k + step], own_ref[:, k : k + step]])
        gate += jnp.dot(part, gate_ref[0, k : k + step], preferred_element_type=jnp.float32)
        up += jnp.dot(part, up_ref[0, k : k + step], preferred_element_type=jnp.float32)
    hidden = (gate / (1.0 + jnp.exp(-gate)) * up).astype(jnp.bfloat16)
    parts = jnp.concatenate([other_ref[:, width:], own_ref[:, width:]]).astype(jnp.float32)
    lane = lax.broadcasted_iota(jnp.int32, (1, extra), 1)
    weight = jnp.sum(jnp.where(lax.rem(lane, owners) == me, parts, 0.0), axis=1, keepdims=True)
    for k in range(0, width, step):
        down = down_ref[0, :, k : k + step]
        value = jnp.dot(hidden, down, preferred_element_type=jnp.float32) * weight
        away_ref[:, k : k + step] = value[:rows].astype(jnp.bfloat16)
        keep_ref[:, k : k + step] = value[rows:]


def diag_kernel(keep_ref, got_ref, left_ref, right_ref):
    span, half = left_ref.shape
    total = keep_ref[3 * span :] + got_ref[3 * span :].astype(jnp.float32)
    left_ref[...] = total[:, :half].astype(jnp.bfloat16)
    right_ref[...] = total[:, half:].astype(jnp.bfloat16)


def plane_kernel(keep_ref, got_ref, left_ref, right_ref, x_ref, y_ref):
    span, half = left_ref.shape
    total = keep_ref[span : 3 * span] + got_ref[span : 3 * span].astype(jnp.float32)
    x_ref[:, :half] = (total[:span, :half] + left_ref[...].astype(jnp.float32)).astype(jnp.bfloat16)
    x_ref[:, half:] = total[:span, half:].astype(jnp.bfloat16)
    y_ref[:, :half] = total[span:, :half].astype(jnp.bfloat16)
    y_ref[:, half:] = (total[span:, half:] + right_ref[...].astype(jnp.float32)).astype(
        jnp.bfloat16
    )


def column_kernel(keep_ref, got_ref, x_ref, y_ref, *out_refs):
    count = out_refs[0].shape[0]
    for i, out_ref in enumerate(out_refs):
        rows = slice(i * count, (i + 1) * count)
        total = keep_ref[rows] + got_ref[rows].astype(jnp.float32)
        total = total + x_ref[rows].astype(jnp.float32) + y_ref[rows].astype(jnp.float32)
        out_ref[...] = total.astype(out_ref.dtype)


def finish_kernel(first_ref, *refs):
    total = first_ref[...]
    for ref in refs[:-1]:
        total = total + ref[...].astype(jnp.float32)
    refs[-1][...] = total.astype(jnp.bfloat16)


def load_kernel(*refs):
    count = len(refs) // 2
    sources, targets, sem = refs[:count], refs[count:-1], refs[-1]
    copies = [pltpu.make_async_copy(*pair, sem.at[i]) for i, pair in enumerate(zip(sources, targets))]
    for copy in copies:
        copy.start()
    for copy in copies:
        copy.wait()


def load(*arrays):
    held = sum(math.prod(x.shape) * x.dtype.itemsize for x in arrays)
    return pl.pallas_call(
        load_kernel,
        out_shape=[jax.ShapeDtypeStruct(x.shape, x.dtype) for x in arrays],
        in_specs=[pl.BlockSpec(memory_space=pl.ANY)] * len(arrays),
        out_specs=[VMEM] * len(arrays),
        scratch_shapes=[pltpu.SemaphoreType.DMA((len(arrays),))],
        compiler_params=pltpu.CompilerParams(vmem_limit_bytes=ROOM - held),
        cost_estimate=pl.CostEstimate(flops=0, bytes_accessed=2 * held, transcendentals=0),
    )(*arrays)


def body(tokens, norm_gain, expert_ids, route_weight, placement, w_gate, w_up, w_down):
    count, width = tokens.shape
    owners = lax.axis_size("dev")
    half = width // 2
    extra = -(-3 * owners // 128) * 128
    bf16, f32 = jnp.bfloat16, jnp.float32
    packed = prepare(tokens, norm_gain, expert_ids, route_weight, placement, owners, extra)
    offsets = list(range(0, owners, 4))
    far = [r for r in offsets if 2 * r >= owners]
    close = [r for r in offsets if 2 * r < owners]
    groups = [group for group in (far, close) if group]
    blocks = {r: swap(packed, "dev", r) for group in groups for r in group if r}
    *weights, blocks[0] = load(w_gate, w_up, w_down, packed)
    blocks, weights = lax.optimization_barrier((blocks, weights))
    pieces = []
    for group in groups:
        column = stack(*[blocks[r] for r in group])
        along_x = swap(column, "dev", 1)
        along_y = swap(column, "dev", 2)
        left = swap(along_y[:, :half], "dev", 1)
        right = swap(along_x[:, half:], "dev", 2)
        rows = 4 * column.shape[0]
        own = local_call(
            collect_kernel, [((rows, width + extra), bf16)], column, along_x, along_y, left, right
        )[0]
        other = swap(own, "side", 1)
        away, keep = local_call(
            expert_kernel,
            [((rows, width), bf16), ((rows, width), f32)],
            own, other, *weights,
        )
        pieces.append((away, keep))
    sums = {}
    for group, (away, keep) in zip(groups, pieces):
        span = len(group) * count
        got = swap(away, "side", 1)
        left, right = local_call(diag_kernel, [((span, half), bf16)] * 2, keep, got)
        left = swap(left, "dev", 2)
        right = swap(right, "dev", 1)
        along_x, along_y = local_call(
            plane_kernel, [((span, width), bf16)] * 2, keep, got, left, right
        )
        along_x = swap(along_x, "dev", 1)
        along_y = swap(along_y, "dev", 2)
        totals = local_call(
            column_kernel,
            [((count, width), bf16 if r else f32) for r in group],
            keep, got, along_x, along_y,
        )
        for r, total in zip(group, totals):
            sums[r] = swap(total, "dev", r) if r else total
    return local_call(finish_kernel, [((count, width), bf16)], *[sums[r] for r in sorted(sums)])[0]


def solution(mesh):
    in_specs = (
        P(("groups", "side", "dev"), None),
        P(),
        P(("groups", "side", "dev"), None),
        P(("groups", "side", "dev"), None),
        P(),
        P("dev", None, "side"),
        P("dev", None, "side"),
        P("dev", "side", None),
    )
    out_specs = P(("groups", "side", "dev"), None)
    return jax.shard_map(body, mesh=mesh, in_specs=in_specs, out_specs=out_specs, check_vma=False)
```

```python
import functools
import math

import jax
import jax.numpy as jnp
from jax import lax
from jax.experimental import pallas as pl
from jax.experimental.pallas import tpu as pltpu
from jax.sharding import PartitionSpec as P


def swap(block, axis, offset):
    count = lax.axis_size(axis)
    return lax.ppermute(block, axis, [(i, i ^ offset) for i in range(count)])


def prepare_kernel(slots, tok_ref, gain_ref, ids_ref, weight_ref, placement_ref, out_ref):
    width = tok_ref.shape[1]
    values = tok_ref[...].astype(jnp.float32)
    scale = lax.rsqrt(jnp.mean(values * values, axis=-1, keepdims=True) + 1e-06)
    out_ref[:, :width] = (values * scale * gain_ref[...].reshape(1, width)).astype(jnp.bfloat16)
    ids = ids_ref[...]
    slot = jnp.zeros_like(ids)
    for expert in range(placement_ref.shape[0]):
        slot = jnp.where(ids == expert, placement_ref[expert], slot)
    lane = lax.broadcasted_iota(jnp.int32, (ids.shape[0], out_ref.shape[1] - width), 1)
    section = sum((lane >= i * slots).astype(jnp.int32) for i in range(1, 4))
    place = lane - section * slots
    mixing = jnp.zeros(lane.shape, jnp.float32)
    for k in range(ids.shape[1]):
        mixing += jnp.where(place == slot[:, k : k + 1], weight_ref[:, k : k + 1], 0.0)
    high = mixing.astype(jnp.bfloat16)
    rest = mixing - high.astype(jnp.float32)
    middle = rest.astype(jnp.bfloat16)
    low = rest - middle.astype(jnp.float32)
    parts = jnp.where(
        section == 0,
        high.astype(jnp.float32),
        jnp.where(section == 1, middle.astype(jnp.float32), jnp.where(section == 2, low, 0.0)),
    )
    out_ref[:, width:] = parts.astype(jnp.bfloat16)


def prepare(tokens, norm_gain, expert_ids, route_weight, placement, slots, extra):
    count, width = tokens.shape
    vmem = pl.BlockSpec(memory_space=pltpu.VMEM)
    return pl.pallas_call(
        functools.partial(prepare_kernel, slots),
        out_shape=jax.ShapeDtypeStruct((count, width + extra), jnp.bfloat16),
        in_specs=[vmem, vmem, vmem, vmem, pl.BlockSpec(memory_space=pltpu.SMEM)],
        out_specs=vmem,
        compiler_params=pltpu.CompilerParams(vmem_limit_bytes=LIMIT),
    )(tokens, norm_gain, expert_ids, route_weight, placement)


VMEM = pl.BlockSpec(memory_space=pltpu.VMEM)
LIMIT = 56 * 1024 * 1024
ROOM = int(53.0 * 1024 * 1024)


def local_call(kernel, outs, *operands, hint=0):
    held = sum(math.prod(x.shape) * x.dtype.itemsize for x in operands)
    held += sum(math.prod(shape) * jnp.dtype(dtype).itemsize for shape, dtype in outs)
    return pl.pallas_call(
        kernel,
        out_shape=[jax.ShapeDtypeStruct(shape, dtype) for shape, dtype in outs],
        in_specs=[VMEM] * len(operands),
        out_specs=[VMEM] * len(outs),
        compiler_params=pltpu.CompilerParams(vmem_limit_bytes=min(LIMIT, 2 * held + (1 << 21))),
        cost_estimate=pl.CostEstimate(flops=0, bytes_accessed=hint or held, transcendentals=0),
    )(*operands)


def stack_kernel(*refs):
    out_ref = refs[-1]
    start = 0
    for ref in refs[:-1]:
        out_ref[start : start + ref.shape[0]] = ref[...]
        start += ref.shape[0]


def stack(*blocks):
    if len(blocks) == 1:
        return blocks[0]
    rows = sum(block.shape[0] for block in blocks)
    return local_call(
        stack_kernel, [((rows, blocks[0].shape[1]), blocks[0].dtype)], *blocks, hint=8 << 20
    )[0]


def collect_kernel(column_ref, x_ref, y_ref, left_ref, right_ref, out_ref):
    span = column_ref.shape[0]
    half = left_ref.shape[1]
    out_ref[:span] = column_ref[...]
    out_ref[span : 2 * span] = x_ref[...]
    out_ref[2 * span : 3 * span] = y_ref[...]
    out_ref[3 * span :, :half] = left_ref[...]
    out_ref[3 * span :, half:] = right_ref[...]


def expert_kernel(own_ref, other_ref, gate_ref, up_ref, down_ref, away_ref, keep_ref):
    rows, width = keep_ref.shape
    extra = own_ref.shape[1] - width
    owners = lax.axis_size("dev")
    me = lax.axis_index("dev")
    step = min(width, 1024)
    gate = up = 0.0
    for k in range(0, width, step):
        part = jnp.concatenate([other_ref[:, k : k + step], own_ref[:, k : k + step]])
        gate += jnp.dot(part, gate_ref[0, k : k + step], preferred_element_type=jnp.float32)
        up += jnp.dot(part, up_ref[0, k : k + step], preferred_element_type=jnp.float32)
    hidden = (gate / (1.0 + jnp.exp(-gate)) * up).astype(jnp.bfloat16)
    parts = jnp.concatenate([other_ref[:, width:], own_ref[:, width:]]).astype(jnp.float32)
    lane = lax.broadcasted_iota(jnp.int32, (1, extra), 1)
    weight = jnp.sum(jnp.where(lax.rem(lane, owners) == me, parts, 0.0), axis=1, keepdims=True)
    for k in range(0, width, step):
        down = down_ref[0, :, k : k + step]
        value = jnp.dot(hidden, down, preferred_element_type=jnp.float32) * weight
        away_ref[:, k : k + step] = value[:rows].astype(jnp.bfloat16)
        keep_ref[:, k : k + step] = value[rows:]


def diag_kernel(keep_ref, got_ref, left_ref, right_ref):
    span, half = left_ref.shape
    total = keep_ref[3 * span :] + got_ref[3 * span :].astype(jnp.float32)
    left_ref[...] = total[:, :half].astype(jnp.bfloat16)
    right_ref[...] = total[:, half:].astype(jnp.bfloat16)


def plane_kernel(keep_ref, got_ref, left_ref, right_ref, x_ref, y_ref):
    span, half = left_ref.shape
    total = keep_ref[span : 3 * span] + got_ref[span : 3 * span].astype(jnp.float32)
    x_ref[:, :half] = (total[:span, :half] + left_ref[...].astype(jnp.float32)).astype(jnp.bfloat16)
    x_ref[:, half:] = total[:span, half:].astype(jnp.bfloat16)
    y_ref[:, :half] = total[span:, :half].astype(jnp.bfloat16)
    y_ref[:, half:] = (total[span:, half:] + right_ref[...].astype(jnp.float32)).astype(
        jnp.bfloat16
    )


def column_kernel(keep_ref, got_ref, x_ref, y_ref, *out_refs):
    count = out_refs[0].shape[0]
    for i, out_ref in enumerate(out_refs):
        rows = slice(i * count, (i + 1) * count)
        total = keep_ref[rows] + got_ref[rows].astype(jnp.float32)
        total = total + x_ref[rows].astype(jnp.float32) + y_ref[rows].astype(jnp.float32)
        out_ref[...] = total.astype(out_ref.dtype)


def finish_kernel(first_ref, *refs):
    total = first_ref[...]
    for ref in refs[:-1]:
        total = total + ref[...].astype(jnp.float32)
    refs[-1][...] = total.astype(jnp.bfloat16)


def load_kernel(*refs):
    count = len(refs) // 2
    sources, targets, sem = refs[:count], refs[count:-1], refs[-1]
    copies = [pltpu.make_async_copy(*pair, sem.at[i]) for i, pair in enumerate(zip(sources, targets))]
    for copy in copies:
        copy.start()
    for copy in copies:
        copy.wait()


def load(*arrays):
    held = sum(math.prod(x.shape) * x.dtype.itemsize for x in arrays)
    return pl.pallas_call(
        load_kernel,
        out_shape=[jax.ShapeDtypeStruct(x.shape, x.dtype) for x in arrays],
        in_specs=[pl.BlockSpec(memory_space=pl.ANY)] * len(arrays),
        out_specs=[VMEM] * len(arrays),
        scratch_shapes=[pltpu.SemaphoreType.DMA((len(arrays),))],
        compiler_params=pltpu.CompilerParams(vmem_limit_bytes=ROOM - held),
        cost_estimate=pl.CostEstimate(flops=0, bytes_accessed=2 * held, transcendentals=0),
    )(*arrays)


def body(tokens, norm_gain, expert_ids, route_weight, placement, w_gate, w_up, w_down):
    count, width = tokens.shape
    owners = lax.axis_size("dev")
    half = width // 2
    extra = -(-3 * owners // 128) * 128
    bf16, f32 = jnp.bfloat16, jnp.float32
    packed = prepare(tokens, norm_gain, expert_ids, route_weight, placement, owners, extra)
    offsets = list(range(0, owners, 4))
    far = [r for r in offsets if 2 * r >= owners]
    close = [r for r in offsets if 2 * r < owners]
    groups = [group for group in (far, close) if group]
    blocks = {r: swap(packed, "dev", r) for group in groups for r in group if r}
    *weights, blocks[0] = load(w_gate, w_up, w_down, packed)
    blocks, weights = lax.optimization_barrier((blocks, weights))
    pieces = []
    for group in groups:
        column = stack(*[blocks[r] for r in group])
        along_x = swap(column, "dev", 1)
        along_y = swap(column, "dev", 2)
        left = swap(along_y[:, :half], "dev", 1)
        right = swap(along_x[:, half:], "dev", 2)
        rows = 4 * column.shape[0]
        own = local_call(
            collect_kernel, [((rows, width + extra), bf16)], column, along_x, along_y, left, right
        )[0]
        other = swap(own, "side", 1)
        away, keep = local_call(
            expert_kernel,
            [((rows, width), bf16), ((rows, width), f32)],
            own, other, *weights,
        )
        pieces.append((away, keep))
    sums = {}
    for group, (away, keep) in zip(groups, pieces):
        span = len(group) * count
        got = swap(away, "side", 1)
        left, right = local_call(diag_kernel, [((span, half), bf16)] * 2, keep, got)
        right = swap(right, "dev", 1)
        left = swap(left, "dev", 2)
        along_x, along_y = local_call(
            plane_kernel, [((span, width), bf16)] * 2, keep, got, left, right
        )
        along_x = swap(along_x, "dev", 1)
        along_y = swap(along_y, "dev", 2)
        totals = local_call(
            column_kernel,
            [((count, width), bf16 if r else f32) for r in group],
            keep, got, along_x, along_y,
        )
        for r, total in zip(group, totals):
            sums[r] = swap(total, "dev", r) if r else total
    return local_call(finish_kernel, [((count, width), bf16)], *[sums[r] for r in sorted(sums)])[0]


def solution(mesh):
    in_specs = (
        P(("groups", "side", "dev"), None),
        P(),
        P(("groups", "side", "dev"), None),
        P(("groups", "side", "dev"), None),
        P(),
        P("dev", None, "side"),
        P("dev", None, "side"),
        P("dev", "side", None),
    )
    out_specs = P(("groups", "side", "dev"), None)
    return jax.shard_map(body, mesh=mesh, in_specs=in_specs, out_specs=out_specs, check_vma=False)
```

```python
import functools
import math

import jax
import jax.numpy as jnp
from jax import lax
from jax.experimental import pallas as pl
from jax.experimental.pallas import tpu as pltpu
from jax.sharding import PartitionSpec as P


def swap(block, axis, offset):
    count = lax.axis_size(axis)
    return lax.ppermute(block, axis, [(i, i ^ offset) for i in range(count)])


def prepare_kernel(slots, tok_ref, gain_ref, ids_ref, weight_ref, placement_ref, out_ref):
    width = tok_ref.shape[1]
    values = tok_ref[...].astype(jnp.float32)
    scale = lax.rsqrt(jnp.mean(values * values, axis=-1, keepdims=True) + 1e-06)
    out_ref[:, :width] = (values * scale * gain_ref[...].reshape(1, width)).astype(jnp.bfloat16)
    ids = ids_ref[...]
    slot = jnp.zeros_like(ids)
    for expert in range(placement_ref.shape[0]):
        slot = jnp.where(ids == expert, placement_ref[expert], slot)
    lane = lax.broadcasted_iota(jnp.int32, (ids.shape[0], out_ref.shape[1] - width), 1)
    place = lax.rem(lane, slots)
    section = lax.div(lane, slots)
    mixing = jnp.zeros(lane.shape, jnp.float32)
    for k in range(ids.shape[1]):
        mixing += jnp.where(place == slot[:, k : k + 1], weight_ref[:, k : k + 1], 0.0)
    high = mixing.astype(jnp.bfloat16)
    rest = mixing - high.astype(jnp.float32)
    middle = rest.astype(jnp.bfloat16)
    low = rest - middle.astype(jnp.float32)
    parts = jnp.where(
        section == 0,
        high.astype(jnp.float32),
        jnp.where(section == 1, middle.astype(jnp.float32), jnp.where(section == 2, low, 0.0)),
    )
    out_ref[:, width:] = parts.astype(jnp.bfloat16)


def prepare(tokens, norm_gain, expert_ids, route_weight, placement, slots, extra):
    count, width = tokens.shape
    vmem = pl.BlockSpec(memory_space=pltpu.VMEM)
    return pl.pallas_call(
        functools.partial(prepare_kernel, slots),
        out_shape=jax.ShapeDtypeStruct((count, width + extra), jnp.bfloat16),
        in_specs=[vmem, vmem, vmem, vmem, pl.BlockSpec(memory_space=pltpu.SMEM)],
        out_specs=vmem,
        compiler_params=pltpu.CompilerParams(vmem_limit_bytes=LIMIT),
    )(tokens, norm_gain, expert_ids, route_weight, placement)


VMEM = pl.BlockSpec(memory_space=pltpu.VMEM)
LIMIT = 56 * 1024 * 1024
ROOM = int(53.0 * 1024 * 1024)


def local_call(kernel, outs, *operands, hint=0):
    held = sum(math.prod(x.shape) * x.dtype.itemsize for x in operands)
    held += sum(math.prod(shape) * jnp.dtype(dtype).itemsize for shape, dtype in outs)
    return pl.pallas_call(
        kernel,
        out_shape=[jax.ShapeDtypeStruct(shape, dtype) for shape, dtype in outs],
        in_specs=[VMEM] * len(operands),
        out_specs=[VMEM] * len(outs),
        compiler_params=pltpu.CompilerParams(vmem_limit_bytes=min(LIMIT, 2 * held + (1 << 21))),
        cost_estimate=pl.CostEstimate(flops=0, bytes_accessed=hint or held, transcendentals=0),
    )(*operands)


def stack_kernel(*refs):
    out_ref = refs[-1]
    start = 0
    for ref in refs[:-1]:
        out_ref[start : start + ref.shape[0]] = ref[...]
        start += ref.shape[0]


def stack(*blocks):
    if len(blocks) == 1:
        return blocks[0]
    rows = sum(block.shape[0] for block in blocks)
    return local_call(
        stack_kernel, [((rows, blocks[0].shape[1]), blocks[0].dtype)], *blocks, hint=8 << 20
    )[0]


def collect_kernel(column_ref, x_ref, y_ref, left_ref, right_ref, out_ref):
    span = column_ref.shape[0]
    half = left_ref.shape[1]
    out_ref[:span] = column_ref[...]
    out_ref[span : 2 * span] = x_ref[...]
    out_ref[2 * span : 3 * span] = y_ref[...]
    out_ref[3 * span :, :half] = left_ref[...]
    out_ref[3 * span :, half:] = right_ref[...]


def expert_kernel(own_ref, other_ref, gate_ref, up_ref, down_ref, away_ref, keep_ref):
    rows, width = keep_ref.shape
    extra = own_ref.shape[1] - width
    owners = lax.axis_size("dev")
    me = lax.axis_index("dev")
    step = min(width, 2048)
    gate = up = 0.0
    for k in range(0, width, step):
        part = jnp.concatenate([other_ref[:, k : k + step], own_ref[:, k : k + step]])
        gate += jnp.dot(part, gate_ref[0, k : k + step], preferred_element_type=jnp.float32)
        up += jnp.dot(part, up_ref[0, k : k + step], preferred_element_type=jnp.float32)
    hidden = (gate / (1.0 + jnp.exp(-gate)) * up).astype(jnp.bfloat16)
    parts = jnp.concatenate([other_ref[:, width:], own_ref[:, width:]]).astype(jnp.float32)
    lane = lax.broadcasted_iota(jnp.int32, (1, extra), 1)
    weight = jnp.sum(jnp.where(lax.rem(lane, owners) == me, parts, 0.0), axis=1, keepdims=True)
    step = min(width, 512)
    for k in range(0, width, step):
        down = down_ref[0, :, k : k + step]
        value = jnp.dot(hidden, down, preferred_element_type=jnp.float32) * weight
        away_ref[:, k : k + step] = value[:rows].astype(jnp.bfloat16)
        keep_ref[:, k : k + step] = value[rows:]


def diag_kernel(keep_ref, got_ref, left_ref, right_ref):
    span, half = left_ref.shape
    total = keep_ref[3 * span :] + got_ref[3 * span :].astype(jnp.float32)
    left_ref[...] = total[:, :half].astype(jnp.bfloat16)
    right_ref[...] = total[:, half:].astype(jnp.bfloat16)


def plane_kernel(keep_ref, got_ref, left_ref, right_ref, x_ref, y_ref):
    span, half = left_ref.shape
    total = keep_ref[span : 3 * span] + got_ref[span : 3 * span].astype(jnp.float32)
    x_ref[:, :half] = (total[:span, :half] + left_ref[...].astype(jnp.float32)).astype(jnp.bfloat16)
    x_ref[:, half:] = total[:span, half:].astype(jnp.bfloat16)
    y_ref[:, :half] = total[span:, :half].astype(jnp.bfloat16)
    y_ref[:, half:] = (total[span:, half:] + right_ref[...].astype(jnp.float32)).astype(
        jnp.bfloat16
    )


def column_kernel(keep_ref, got_ref, x_ref, y_ref, *out_refs):
    count = out_refs[0].shape[0]
    for i, out_ref in enumerate(out_refs):
        rows = slice(i * count, (i + 1) * count)
        total = keep_ref[rows] + got_ref[rows].astype(jnp.float32)
        total = total + x_ref[rows].astype(jnp.float32) + y_ref[rows].astype(jnp.float32)
        out_ref[...] = total.astype(out_ref.dtype)


def finish_kernel(first_ref, *refs):
    total = first_ref[...]
    for ref in refs[:-1]:
        total = total + ref[...].astype(jnp.float32)
    refs[-1][...] = total.astype(jnp.bfloat16)


def load_kernel(*refs):
    count = len(refs) // 2
    sources, targets, sem = refs[:count], refs[count:-1], refs[-1]
    copies = [pltpu.make_async_copy(*pair, sem.at[i]) for i, pair in enumerate(zip(sources, targets))]
    for copy in copies:
        copy.start()
    for copy in copies:
        copy.wait()


def load(*arrays):
    held = sum(math.prod(x.shape) * x.dtype.itemsize for x in arrays)
    return pl.pallas_call(
        load_kernel,
        out_shape=[jax.ShapeDtypeStruct(x.shape, x.dtype) for x in arrays],
        in_specs=[pl.BlockSpec(memory_space=pl.ANY)] * len(arrays),
        out_specs=[VMEM] * len(arrays),
        scratch_shapes=[pltpu.SemaphoreType.DMA((len(arrays),))],
        compiler_params=pltpu.CompilerParams(vmem_limit_bytes=ROOM - held),
        cost_estimate=pl.CostEstimate(flops=0, bytes_accessed=2 * held, transcendentals=0),
    )(*arrays)


def body(tokens, norm_gain, expert_ids, route_weight, placement, w_gate, w_up, w_down):
    count, width = tokens.shape
    owners = lax.axis_size("dev")
    half = width // 2
    extra = -(-3 * owners // 128) * 128
    bf16, f32 = jnp.bfloat16, jnp.float32
    packed = prepare(tokens, norm_gain, expert_ids, route_weight, placement, owners, extra)
    offsets = list(range(0, owners, 4))
    far = [r for r in offsets if 2 * r >= owners]
    close = [r for r in offsets if 2 * r < owners]
    groups = [group for group in (far, close) if group]
    blocks = {r: swap(packed, "dev", r) for group in groups for r in group if r}
    *weights, blocks[0] = load(w_gate, w_up, w_down, packed)
    blocks, weights = lax.optimization_barrier((blocks, weights))
    pieces = []
    for group in groups:
        column = stack(*[blocks[r] for r in group])
        along_x = swap(column, "dev", 1)
        along_y = swap(column, "dev", 2)
        left = swap(along_y[:, :half], "dev", 1)
        right = swap(along_x[:, half:], "dev", 2)
        rows = 4 * column.shape[0]
        own = local_call(
            collect_kernel, [((rows, width + extra), bf16)], column, along_x, along_y, left, right
        )[0]
        other = swap(own, "side", 1)
        away, keep = local_call(
            expert_kernel,
            [((rows, width), bf16), ((rows, width), f32)],
            own, other, *weights,
        )
        pieces.append((away, keep))
    sums = {}
    for group, (away, keep) in zip(groups, pieces):
        span = len(group) * count
        got = swap(away, "side", 1)
        left, right = local_call(diag_kernel, [((span, half), bf16)] * 2, keep, got)
        left = swap(left, "dev", 2)
        right = swap(right, "dev", 1)
        along_x, along_y = local_call(
            plane_kernel, [((span, width), bf16)] * 2, keep, got, left, right
        )
        along_x = swap(along_x, "dev", 1)
        along_y = swap(along_y, "dev", 2)
        totals = local_call(
            column_kernel,
            [((count, width), bf16 if r else f32) for r in group],
            keep, got, along_x, along_y,
        )
        for r, total in zip(group, totals):
            sums[r] = swap(total, "dev", r) if r else total
    return local_call(finish_kernel, [((count, width), bf16)], *[sums[r] for r in sorted(sums)])[0]


def solution(mesh):
    in_specs = (
        P(("groups", "side", "dev"), None),
        P(),
        P(("groups", "side", "dev"), None),
        P(("groups", "side", "dev"), None),
        P(),
        P("dev", None, "side"),
        P("dev", None, "side"),
        P("dev", "side", None),
    )
    out_specs = P(("groups", "side", "dev"), None)
    return jax.shard_map(body, mesh=mesh, in_specs=in_specs, out_specs=out_specs, check_vma=False)
```
